128 devices in a mesh: dp: 8 (over y, z_lo), seq: 16 (over x, z_hi, core).
Axes of the slice: x: 4, y: 4, z: 4 (z_hi: 2, z_lo: 2; z = z_hi * 2 + z_lo), core: 2. Of those that a mesh axis runs over, the one named last changes fastest.
Arguments:
- normed: bfloat16 [8, 4096, 1536], P('dp', 'seq'), may hold values from -12 to 12
- w_query: bfloat16 [1536, 768], replicated, may hold values from -0.15309311 to 0.15309311
- w_key: bfloat16 [1536, 768], replicated, may hold values from -0.15309311 to 0.15309311
- w_value: bfloat16 [1536, 768], replicated, may hold values from -0.15625 to 0.15625
- grad_context: bfloat16 [8, 4096, 768], P('dp', 'seq'), may hold values from -6 to 6
Outputs:
- d_normed: bfloat16 [8, 4096, 1536], P('dp', 'seq')
- grad_query: float32 [1536, 768], P(('dp', 'seq'))
- grad_key: float32 [1536, 768], P(('dp', 'seq'))
- grad_value: float32 [1536, 768], P(('dp', 'seq'))
The draws below stay inside these ranges and needn't reach their ends.
All inputs are finite; a program needn't handle non-finite values.
Results may differ from the reference program's by a relative error of at most 0.017.
Values may be sent and summed in bfloat16 or wider, within the bound.
No kernel may reach another device: no remote copies, remote signals or barrier semaphores. Data moves between devices by JAX's collectives and lax.ppermute only.
A program may use at most 192 MiB of HBM per device.

```python
import math
import jax
import jax.numpy as jnp
from jax import lax

D = 1536
H = 4
E = 192
QS = 256
HD = 768
L = 4096
SAMPLES = 8
N_SEQ = 16


def base_weight(key):
    values = jnp.clip(jax.random.normal(key, (D, H * E), jnp.float32), -6.0, 6.0)
    return values / jnp.sqrt(jnp.float32(D))


def draw_w_query(key, part):
    shared = base_weight(key)
    return shared.astype(jnp.bfloat16)


def draw_w_key(key, part):
    key = jax.random.fold_in(key, 12)
    own = base_weight(key)
    mixed = own
    return mixed.astype(jnp.bfloat16)


def draw_normed(key, part):
    key = jax.random.fold_in(key, 13)
    keys = jax.random.split(key, 2)
    values = jnp.clip(jax.random.normal(keys[1], (SAMPLES, L, D), jnp.float32), -6.0, 6.0)
    return values.astype(jnp.bfloat16)


def level_of(own_key, dims, cuts, smallest, largest):
    def one(dim, blocks):
        heights = jax.random.uniform(jax.random.fold_in(jax.random.fold_in(own_key, 6), dim), (blocks,), jnp.float32, smallest / len(cuts), largest / len(cuts))
        return jnp.repeat(jnp.exp(heights), dims[dim] // blocks).reshape((-1,) + (1,) * (len(dims) - dim - 1))

    loudness = one(*cuts[0])
    for cut in cuts[1:]:
        loudness = loudness * one(*cut)
    return loudness


def scatter_about(rng, shape, scale, bound, cuts=(), kind=jnp.bfloat16):
    level = level_of(rng, shape, cuts, -0.22, 0.18) if cuts else 1.0
    result = jax.random.normal(rng, shape, jnp.float32) * scale * level
    return jnp.minimum(jnp.maximum(result, -bound), bound).astype(kind)


def setup_inputs(seed: int = 0) -> dict:
    streams_of = jax.random.split(jax.random.key(seed), 6)
    normed = draw_normed(jax.random.fold_in(streams_of[5], 71), 0)
    w_query = draw_w_query(jax.random.fold_in(streams_of[5], 71), 0)
    w_key = draw_w_key(jax.random.fold_in(streams_of[5], 71), 0)
    w_value = scatter_about(streams_of[3], (D, HD), D ** -0.5, 0.15625)
    grad_context = scatter_about(streams_of[4], (SAMPLES, L, HD), 1.0, 6.0, ((0, 8), (1, 16)))
    return dict(normed=normed, w_query=w_query, w_key=w_key, w_value=w_value, grad_context=grad_context)


def project(rows, weight):
    return jnp.dot(rows, weight, preferred_element_type=jnp.float32).astype(jnp.bfloat16)

def rounded_sum(partials):
    kept = lax.optimization_barrier(partials.astype(jnp.bfloat16))
    return lax.optimization_barrier(jnp.sum(kept.astype(jnp.float32), axis=0)).astype(jnp.bfloat16)

def reference(normed, w_query, w_key, w_value, grad_context):
    scale = 1.0 / math.sqrt(E)

    def one_sample(pair):
        rows, cot_rows = pair
        query = project(rows, w_query).astype(jnp.float32).reshape(L, H, E)
        key = project(rows, w_key).astype(jnp.float32).reshape(L, H, E)
        value = project(rows, w_value).astype(jnp.float32).reshape(L, H, E)
        cotan = cot_rows.astype(jnp.float32).reshape(L, H, E)
        scores = jnp.einsum('qhe,khe->hqk', query, key) * scale
        probs = jax.nn.softmax(scores, axis=-1)
        dprob = jnp.einsum('qhe,khe->hqk', cotan, value)
        delta = lax.optimization_barrier(jnp.sum(probs * dprob, axis=-1, keepdims=True))
        dscore = lax.optimization_barrier((probs * (dprob - delta) * scale).astype(jnp.bfloat16)).astype(jnp.float32)
        prob_b = lax.optimization_barrier(probs.astype(jnp.bfloat16)).astype(jnp.float32)
        dq = rounded_sum(jnp.einsum('hqnk,nkhe->nqhe', dscore.reshape(H, L, N_SEQ, QS), key.reshape(N_SEQ, QS, H, E))).reshape(L, H * E)
        dk = rounded_sum(jnp.einsum('hnqk,nqhe->nkhe', dscore.reshape(H, N_SEQ, QS, L), query.reshape(N_SEQ, QS, H, E))).reshape(L, H * E)
        dv = rounded_sum(jnp.einsum('hnqk,nqhe->nkhe', prob_b.reshape(H, N_SEQ, QS, L), cotan.reshape(N_SEQ, QS, H, E))).reshape(L, H * E)
        back = jnp.dot(dq, w_query.T, preferred_element_type=jnp.float32)
        back = back + jnp.dot(dk, w_key.T, preferred_element_type=jnp.float32)
        back = back + jnp.dot(dv, w_value.T, preferred_element_type=jnp.float32)
        grad_q = jnp.dot(rows.T, dq, preferred_element_type=jnp.float32)
        grad_k = jnp.dot(rows.T, dk, preferred_element_type=jnp.float32)
        grad_v = jnp.dot(rows.T, dv, preferred_element_type=jnp.float32)
        return (back.astype(jnp.bfloat16), grad_q, grad_k, grad_v)
    back, grad_q, grad_k, grad_v = lax.map(one_sample, (normed, grad_context))
    return (back, lax.optimization_barrier(jnp.sum(grad_q, axis=0)), lax.optimization_barrier(jnp.sum(grad_k, axis=0)), lax.optimization_barrier(jnp.sum(grad_v, axis=0)))
```

```python
import functools
import math

import jax
import jax.numpy as jnp
from jax import lax
from jax.experimental import pallas as pl
from jax.experimental.pallas import tpu as pltpu
from jax.sharding import Mesh, PartitionSpec as P

F32, BF16 = jnp.float32, jnp.bfloat16
D = 1536
H = 4
E = 192
HD = H * E
NB = 256
NQ = 4 * NB
NK = 16 * NB
KC = 512
SCALE = 1.0 / math.sqrt(E)
C2 = SCALE * math.log2(math.e)
ANY = pl.BlockSpec(memory_space=pl.ANY)
VM = pl.BlockSpec(memory_space=pltpu.VMEM)
SM = pl.BlockSpec(memory_space=pltpu.SMEM)
PARAMS = pltpu.CompilerParams(vmem_limit_bytes=56 * 2**20)
sds = jax.ShapeDtypeStruct


def dot(a, b, dims=(((1,), (0,)), ((), ()))):
    return lax.dot_general(a, b, dims, preferred_element_type=F32)


def nt(a, b):
    return dot(a, b, (((1,), (1,)), ((), ())))


def joined(a, b):
    return jnp.concatenate([a[:, :128], a[:, 128:] + b[:, :128], b[:, 128:]], 1)


def scatter_heads(me, a, b, outs):
    for h in range(H):
        piece = jnp.concatenate([a[:, h * E:(h + 1) * E], b[:, h * E:(h + 1) * E]], 1)
        slot = lax.rem(h - me + H, H)
        for j in range(H):
            @pl.when(slot == j)
            def _(j=j, piece=piece):
                outs[j][...] = piece


KP = D // 4


def projkv_body(me, x, wk, wv, o0, o1, o2, o3, wks, wvs, sem):
    cps = []
    for i in range(4):
        r = pl.ds(i * KP, KP)
        cps.append((pltpu.make_async_copy(wk.at[r], wks.at[r], sem.at[i]),
                    pltpu.make_async_copy(wv.at[r], wvs.at[r], sem.at[4 + i])))
    for a, b in cps:
        a.start()
        b.start()
    k = v = None
    for i in range(4):
        for c in cps[i]:
            c.wait()
        r = pl.ds(i * KP, KP)
        xi = x[:, r]
        dk, dv = dot(xi, wks[r, :]), dot(xi, wvs[r, :])
        k, v = (dk, dv) if i == 0 else (k + dk, v + dv)
    scatter_heads(me[0], k.astype(BF16), v.astype(BF16), (o0, o1, o2, o3))


def projkv(me, x, wk, wv):
    return pl.pallas_call(
        projkv_body, in_specs=[SM, VM, ANY, ANY], out_specs=[VM] * 4,
        out_shape=[sds((NB, 2 * E), BF16)] * 4,
        scratch_shapes=[pltpu.VMEM((D, HD), BF16), pltpu.VMEM((D, HD), BF16),
                        pltpu.SemaphoreType.DMA((8,))],
        compiler_params=PARAMS, name="projkv",
        cost_estimate=pl.CostEstimate(flops=4 * NB * D * HD, bytes_accessed=6 * 2**20, transcendentals=0),
    )(me, x, wk, wv)


def projq_body(me, x, wq, do, o0, o1, o2, o3, wqs, sem):
    cps = []
    for i in range(4):
        r = pl.ds(i * KP, KP)
        cps.append(pltpu.make_async_copy(wq.at[r], wqs.at[r], sem.at[i]))
        cps[i].start()
    q = None
    for i in range(4):
        cps[i].wait()
        r = pl.ds(i * KP, KP)
        dq = dot(x[:, r], wqs[r, :])
        q = dq if i == 0 else q + dq
    scatter_heads(me[0], q.astype(BF16), do[...], (o0, o1, o2, o3))


def projq(me, x, wq, do):
    return pl.pallas_call(
        projq_body, in_specs=[SM, VM, ANY, VM], out_specs=[VM] * 4,
        out_shape=[sds((NB, 2 * E), BF16)] * 4,
        scratch_shapes=[pltpu.VMEM((D, HD), BF16), pltpu.SemaphoreType.DMA((4,))],
        compiler_params=PARAMS, name="projq",
        cost_estimate=pl.CostEstimate(flops=2 * NB * D * HD, bytes_accessed=4 * 2**20, transcendentals=0),
    )(me, x, wq, do)

def attn1_body(*refs):
    kv_in=refs[:16]; qdo_in=refs[16:20]
    rsame, rother, p_out, ds_out, qs_out, dos_out, cq_out, kv_out = refs[20:28]
    kv, qdo, qT, doT, s_scr, dp_scr, p_scr, ds_scr, qs, dos, sem, osem = refs[28:]
    cps=[]
    for i in range(4):
        cps.append(pltpu.make_async_copy(qdo_in[i], qdo.at[pl.ds(256*i,256)], sem.at[i]))
    for i in range(16):
        cps.append(pltpu.make_async_copy(kv_in[i], kv.at[pl.ds(256*i,256)], sem.at[4+i]))
    for c in cps: c.start()
    for c in cps: c.wait()
    kvo=pltpu.make_async_copy(kv, kv_out, osem.at[9]); kvo.start()
    lane=lax.broadcasted_iota(jnp.int32,(256,NQ),0)
    x=qdo[...]
    xT=x.T
    qT[...]=jnp.concatenate([xT[:192], jnp.zeros((64,NQ),BF16)],0)
    doT[...]=jnp.concatenate([jnp.zeros((64,NQ),BF16), xT[192:]],0)
    outs=[]
    NC=NK//KC
    for t in range(4):
        qcol=pl.ds(256*t,256)
        qTt=qT[:,qcol]; doTt=doT[:,qcol]
        def pa(i,m):
            r=pl.ds(pl.multiple_of(i*KC,KC),KC)
            s=dot(kv[r,0:256],qTt)
            s_scr[r,:]=s
            return jnp.maximum(m, jnp.max(s.reshape(KC//8,8,256),axis=0))
        m8=lax.fori_loop(0,NC,pa,jnp.full((8,256),-jnp.inf,F32))
        mc=jnp.max(m8,axis=0,keepdims=True)*C2
        def pb(i,lr):
            l,r_=lr
            r=pl.ds(pl.multiple_of(i*KC,KC),KC)
            dp=dot(kv[r,128:384],doTt)
            p=jnp.exp2(s_scr[r,:]*C2-mc)
            dp_scr[r,:]=dp
            s_scr[r,:]=p
            p_scr[r,qcol]=p.astype(BF16)
            l=l+jnp.sum(p.reshape(KC//8,8,256),axis=0)
            r_=r_+jnp.sum((p*dp).reshape(KC//8,8,256),axis=0)
            return l,r_
        z=jnp.zeros((8,256),F32)
        l8,r8=lax.fori_loop(0,NC,pb,(z,z))
        l=jnp.sum(l8,axis=0,keepdims=True); rr=jnp.sum(r8,axis=0,keepdims=True)
        inv=1.0/l
        delta=rr*inv
        def pc(i,_):
            r=pl.ds(pl.multiple_of(i*KC,KC),KC)
            ds_scr[r,qcol]=(s_scr[r,:]*(dp_scr[r,:]-delta)).astype(BF16)
            return 0
        lax.fori_loop(0,NC,pc,0)
        cq=inv*SCALE
        cq_out[:,qcol]=jnp.broadcast_to(cq,(8,256))
        invc=jnp.broadcast_to(inv,(8,256)).T[:,0:1]
        rows=pl.ds(256*t,256)
        qt=qdo[rows,0:192].astype(F32)*(invc*SCALE)
        dt=qdo[rows,192:384].astype(F32)*invc
        zz=jnp.zeros((256,64),BF16)
        qs[rows,:]=jnp.concatenate([qt.astype(BF16),zz],1)
        dos[rows,:]=jnp.concatenate([zz,dt.astype(BF16)],1)
        o1=pltpu.make_async_copy(ds_scr.at[:,qcol], ds_out.at[:,qcol], osem.at[t]); o1.start()
        o2=pltpu.make_async_copy(p_scr.at[pl.ds(0,2048),qcol], p_out.at[:,qcol], osem.at[4+t]); o2.start()
        outs+= [o1,o2]
    qs_out[...]=qs[...]; dos_out[...]=dos[...]
    for i in range(4):
        r=pl.ds(2048+i*512,512)
        a=dot(ds_scr[r,:],qs[...]); b=dot(p_scr[r,:],dos[...])
        o=jnp.concatenate([a[:,:128],a[:,128:]+b[:,:128],b[:,128:]],1)
        if i<2: rsame[pl.ds(i*512,512),:]=o
        else: rother[pl.ds((i-2)*512,512),:]=o.astype(BF16)
    for o in outs: o.wait()
    kvo.wait()

def attn1(kvp,qdop):
    A, V = ANY, VM
    return pl.pallas_call(attn1_body,
      in_specs=[A]*20,
      out_specs=[V,V,A,A,V,V,V,A],
      out_shape=[sds((1024,384),F32),sds((1024,384),BF16),sds((2048,NQ),BF16),sds((NK,NQ),BF16),sds((NQ,256),BF16),sds((NQ,256),BF16),sds((8,NQ),F32),sds((NK,384),BF16)],
      scratch_shapes=[pltpu.VMEM((NK,384),BF16),pltpu.VMEM((NQ,384),BF16),pltpu.VMEM((256,NQ),BF16),pltpu.VMEM((256,NQ),BF16),
        pltpu.VMEM((NK,256),F32),pltpu.VMEM((NK,256),F32),pltpu.VMEM((NK,NQ),BF16),pltpu.VMEM((NK,NQ),BF16),pltpu.VMEM((NQ,256),BF16),pltpu.VMEM((NQ,256),BF16),
        pltpu.SemaphoreType.DMA((20,)),pltpu.SemaphoreType.DMA((10,))],
      compiler_params=PARAMS,
      name="attn1", cost_estimate=pl.CostEstimate(flops=20*2**30, bytes_accessed=20*2**20, transcendentals=4*2**20),
    )(*kvp,*qdop)

def attn2_body(p_in, ds_in, qs, dos, cq, kv_in, lsame, lother, d0, d1, d2, d3, kv, p, ds, sem):
    cps=[pltpu.make_async_copy(p_in.at[pl.ds(512*i,512)],p.at[pl.ds(512*i,512)],sem.at[i]) for i in range(4)]
    cds=[pltpu.make_async_copy(ds_in.at[pl.ds(512*i,512)],ds.at[pl.ds(512*i,512)],sem.at[4+i]) for i in range(8)]
    ck=pltpu.make_async_copy(kv_in,kv,sem.at[12])
    for i in range(4): cds[i].start(); cps[i].start()
    ck.start()
    for i in range(4,8): cds[i].start()
    for i in (2,3,0,1):
        cds[i].wait(); cps[i].wait()
        r=pl.ds(i*512,512)
        a=dot(ds[r,:],qs[...]); b=dot(p[r,:],dos[...])
        o=jnp.concatenate([a[:,:128],a[:,128:]+b[:,:128],b[:,128:]],1)
        if i<2: lsame[pl.ds(i*512,512),:]=o
        else: lother[pl.ds((i-2)*512,512),:]=o.astype(BF16)
    ck.wait()
    for i in range(4,8): cds[i].wait()
    acc=jnp.zeros((256,NQ),F32)
    for i in range(4):
        r=pl.ds(i*1024,1024)
        kT=kv[r,0:256].T
        acc=acc+dot(kT,ds[r,:])
    dqT=(acc*cq[0:1,:]).astype(BF16)[:192]
    for j, o in enumerate((d0, d1, d2, d3)):
        o[...]=dqT[:, j*NB:(j+1)*NB]

def attn2(p,ds,qs,dos,cq,kv):
    A, V = ANY, VM
    return pl.pallas_call(attn2_body,
      in_specs=[A,A,V,V,V,A], out_specs=[V]*6,
      out_shape=[sds((1024,384),F32),sds((1024,384),BF16),*[sds((E,NB),BF16)]*4],
      scratch_shapes=[pltpu.VMEM((NK,384),BF16),pltpu.VMEM((2048,NQ),BF16),pltpu.VMEM((NK,NQ),BF16),pltpu.SemaphoreType.DMA((13,))],
      compiler_params=PARAMS,
      name="attn2", cost_estimate=pl.CostEstimate(flops=8*2**30, bytes_accessed=16*2**20, transcendentals=0),
    )(p,ds,qs,dos,cq,kv)


def gq_body(core, d0, d1, d2, d3, x0, x1, x2, x3, mine, other):
    acc = None
    c = core[0]
    for d, x in ((d0, x0), (d1, x1), (d2, x2), (d3, x3)):
        g = dot(d[...], x[...])
        acc = g if acc is None else acc + g
    half = E // 2
    for k in range(2):
        @pl.when(c == k)
        def _(k=k):
            mine[...] = acc[k * half:(k + 1) * half]
            other[...] = acc[(1 - k) * half:(2 - k) * half].astype(BF16)


def gq(core, ds, xs):
    return pl.pallas_call(
        gq_body, in_specs=[SM] + [VM] * 8, out_specs=[VM] * 2,
        out_shape=[sds((E // 2, D), F32), sds((E // 2, D), BF16)],
        compiler_params=PARAMS, name="gq",
        cost_estimate=pl.CostEstimate(flops=2 * NQ * D * E, bytes_accessed=5 * 2**20, transcendentals=0),
    )(core, *ds, *xs)


def comb_body(a, t, u, o0, o1, o2, o3):
    for j, o in enumerate((o0, o1, o2, o3)):
        r = pl.ds(j * NB, NB)
        o[...] = (a[r, :] + t[r, :].astype(F32) + u[r, :].astype(F32)).astype(BF16)


def comb(a, t, u):
    return pl.pallas_call(
        comb_body, in_specs=[VM] * 3, out_specs=[VM] * 4, out_shape=[sds((NB, 2 * E), BF16)] * 4,
        compiler_params=PARAMS, name="comb",
        cost_estimate=pl.CostEstimate(flops=2**20, bytes_accessed=4 * 2**20, transcendentals=0),
    )(a, t, u)


def gkv_body(core, d0, d1, d2, d3, x0, x1, x2, x3, mine, other):
    acc = None
    c = core[0]
    for d, x in ((d0, x0), (d1, x1), (d2, x2), (d3, x3)):
        g = dot(d[...].T, x[...])
        acc = g if acc is None else acc + g
    for k in range(2):
        @pl.when(c == k)
        def _(k=k):
            mine[...] = acc[k * E:(k + 1) * E]
            other[...] = acc[(1 - k) * E:(2 - k) * E].astype(BF16)


def gkv(core, ds, xs):
    return pl.pallas_call(
        gkv_body, in_specs=[SM] + [VM] * 8, out_specs=[VM] * 2,
        out_shape=[sds((E, D), F32), sds((E, D), BF16)],
        compiler_params=PARAMS, name="gkv",
        cost_estimate=pl.CostEstimate(flops=4 * NQ * D * E, bytes_accessed=6 * 2**20, transcendentals=0),
    )(core, *ds, *xs)


def split_body(me, a, t, o0, o1, o2, o3):
    w = D // 4
    for j, o in enumerate((o0, o1, o2, o3)):
        at = pl.multiple_of(lax.rem(me[0] + j, 4) * w, 128)
        o[...] = (a[:, pl.ds(at, w)] + t[:, pl.ds(at, w)].astype(F32)).astype(BF16)


def split(me, a, t):
    n = a.shape[0]
    return pl.pallas_call(
        split_body, in_specs=[SM, VM, VM], out_specs=[VM] * 4, out_shape=[sds((n, D // 4), BF16)] * 4,
        compiler_params=PARAMS, name="split",
        cost_estimate=pl.CostEstimate(flops=2**20, bytes_accessed=2 * 2**20, transcendentals=0),
    )(me, a, t)


def back_body(me, q0, q1, q2, q3, p0, p1, p2, p3, wq, wk, wv, out, dqT, dk, dv, wqs, wks, wvs, sem):
    cps = [pltpu.make_async_copy(a, b, sem.at[i]) for i, (a, b) in enumerate(((wq, wqs), (wk, wks), (wv, wvs)))]
    for c in cps:
        c.start()
    m = me[0]
    for j, (q, p) in enumerate(((q0, p0), (q1, p1), (q2, p2), (q3, p3))):
        h = lax.rem(m + j, H)
        dqT[pl.ds(pl.multiple_of(h * E, E), E), :] = q[...]
        for k in range(H):
            @pl.when(h == k)
            def _(k=k, p=p):
                dk[:, k * E:(k + 1) * E] = p[:, :E]
                dv[:, k * E:(k + 1) * E] = p[:, E:]
    cps[0].wait()
    acc = nt(dqT[...].T, wqs[...])
    cps[1].wait()
    acc = acc + nt(dk[...], wks[...])
    cps[2].wait()
    acc = acc + nt(dv[...], wvs[...])
    out[...] = acc.astype(BF16)


def back(me, qs, ps, wq, wk, wv):
    return pl.pallas_call(
        back_body, in_specs=[SM] + [VM] * 8 + [ANY] * 3, out_specs=VM, out_shape=sds((NB, D), BF16),
        scratch_shapes=[pltpu.VMEM((HD, NB), BF16), pltpu.VMEM((NB, HD), BF16), pltpu.VMEM((NB, HD), BF16)]
        + [pltpu.VMEM((D, HD), BF16)] * 3 + [pltpu.SemaphoreType.DMA((3,))],
        compiler_params=PARAMS, name="back",
        cost_estimate=pl.CostEstimate(flops=6 * NB * D * HD, bytes_accessed=9 * 2**20, transcendentals=0),
    )(me, *qs, *ps, wq, wk, wv)


def ahead(x, axis, j, n):
    return lax.ppermute(x, axis, [(i, (i + j) % n) for i in range(n)])


def shards(normed, w_query, w_key, w_value, grad_context):
    rows = normed[0]
    cot = grad_context[0]
    mx = lax.axis_index("x").reshape(1)
    my = lax.axis_index("y").reshape(1)
    mc = lax.axis_index("c").reshape(1)
    kv = projkv(mx, rows, w_key, w_value)
    kv = [kv[0]] + [ahead(kv[j], "x", j, 4) for j in (1, 2, 3)]
    qdo = projq(mx, rows, w_query, cot)
    qdo = [qdo[0]] + [ahead(qdo[j], "x", j, 4) for j in (1, 2, 3)]
    rows2, _ = lax.optimization_barrier((rows, tuple(qdo[1:])))
    xs = [rows] + [ahead(rows2, "x", j, 4) for j in (1, 2, 3)]
    far = [ahead(p, "zh", 1, 2) for p in kv]
    near = [ahead(p, "c", 1, 2) for p in kv]
    diag = [ahead(p, "c", 1, 2) for p in far]
    rsame, rother, p, ds, qs, dos, cq, kvh = attn1(kv + near + far + diag, qdo)
    t = ahead(rother, "c", 1, 2)
    u = ahead((rsame + t.astype(F32)).astype(BF16), "zh", 1, 2)
    lsame, lother, *dqT = attn2(p, ds, qs, dos, cq, kvh)
    t2 = ahead(lother, "c", 1, 2)
    backq = [dqT[0]] + [ahead(dqT[j], "x", 4 - j, 4) for j in (1, 2, 3)]
    gqm, gqo = gq(mc, dqT, xs)
    q4 = split(my, gqm, ahead(gqo, "c", 1, 2))
    q4 = [q4[0]] + [ahead(q4[j], "y", j, 4) for j in (1, 2, 3)]
    dkv = comb(lsame, t2, u)
    backp = [dkv[0]] + [ahead(dkv[j], "x", 4 - j, 4) for j in (1, 2, 3)]
    gm, go = gkv(mc, dkv, xs)
    s4 = split(my, gm, ahead(go, "c", 1, 2))
    s4 = [s4[0]] + [ahead(s4[j], "y", j, 4) for j in (1, 2, 3)]
    d_normed = back(mx, backq, backp, w_query, w_key, w_value).reshape(normed.shape)
    sq = (q4[0].astype(F32) + q4[1].astype(F32)) + (q4[2].astype(F32) + q4[3].astype(F32))
    skv = (s4[0].astype(F32) + s4[1].astype(F32)) + (s4[2].astype(F32) + s4[3].astype(F32))
    s = jnp.concatenate([skv, sq], 0).astype(BF16)
    s = s.T.reshape(32, 12, 288)
    s = lax.all_to_all(s, ("zl", "x", "zh", "c"), 0, 0, tiled=True)
    s = s.astype(F32).reshape(2, 4, 2, 2, 12, 288).sum(axis=(0, 2))
    g = s.transpose(2, 0, 1, 3)
    grad_q = g[..., E:].reshape(12, HD)
    grad_k = g[:, :, 0, :E].reshape(12, HD)
    grad_v = g[:, :, 1, :E].reshape(12, HD)
    return d_normed, grad_q, grad_k, grad_v


def solution(mesh):
    split_mesh = Mesh(mesh.devices.reshape(4, 2, 4, 2, 2), ("y", "zl", "x", "zh", "c"))
    dp, seq = ("y", "zl"), ("x", "zh", "c")
    rows = P(dp, seq, None)
    grads = P(dp + seq, None)
    return jax.shard_map(
        shards, mesh=split_mesh, in_specs=(rows, P(), P(), P(), rows),
        out_specs=(rows, grads, grads, grads), check_vma=False,
    )
```

```python
import functools
import math

import jax
import jax.numpy as jnp
from jax import lax
from jax.experimental import pallas as pl
from jax.experimental.pallas import tpu as pltpu
from jax.sharding import Mesh, PartitionSpec as P

F32, BF16 = jnp.float32, jnp.bfloat16
D = 1536
H = 4
E = 192
HD = H * E
NB = 256
NQ = 4 * NB
NK = 16 * NB
KC = 512
SCALE = 1.0 / math.sqrt(E)
C2 = SCALE * math.log2(math.e)
ANY = pl.BlockSpec(memory_space=pl.ANY)
VM = pl.BlockSpec(memory_space=pltpu.VMEM)
SM = pl.BlockSpec(memory_space=pltpu.SMEM)
PARAMS = pltpu.CompilerParams(vmem_limit_bytes=58 * 2**20)
SMALL = pltpu.CompilerParams(vmem_limit_bytes=24 * 2**20)
sds = jax.ShapeDtypeStruct


def dot(a, b, dims=(((1,), (0,)), ((), ()))):
    return lax.dot_general(a, b, dims, preferred_element_type=F32)


def nt(a, b):
    return dot(a, b, (((1,), (1,)), ((), ())))


def call(body, name, us, ins, outs, out_specs, in_specs=None, scratch=(), params=PARAMS):
    return pl.pallas_call(
        body, in_specs=in_specs or [VM] * len(ins), out_specs=out_specs, out_shape=outs,
        scratch_shapes=list(scratch), compiler_params=params, name=name,
        cost_estimate=pl.CostEstimate(flops=2**20, bytes_accessed=int(us * 1e5), transcendentals=0),
    )(*ins)


KP = D // 4


def send_out(me, scr, outs, sem):
    cps = [pltpu.make_async_copy(scr.at[lax.rem(me + j, H)], outs[j], sem.at[j]) for j in range(4)]
    for c in cps:
        c.start()
    for c in cps:
        c.wait()


def loads(pairs, sem):
    cps = []
    for n, (a, b) in enumerate(pairs):
        for i in range(4):
            r = pl.ds(i * KP, KP)
            cps.append(pltpu.make_async_copy(a.at[r], b.at[r], sem.at[4 * n + i]))
    return cps


TT = (((0,), (1,)), ((), ()))


def projkv_body(me, x, wk, wv, o0, o1, o2, o3, wks, wvs, scr, sem, osem):
    cps = loads(((wk, wks), (wv, wvs)), sem)
    for i in range(4):
        cps[i].start()
        cps[4 + i].start()
    k = v = None
    for i in range(4):
        cps[i].wait()
        cps[4 + i].wait()
        r = pl.ds(i * KP, KP)
        xi = x[:, r]
        dk, dv = dot(wks[r, :], xi, TT), dot(wvs[r, :], xi, TT)
        k, v = (dk, dv) if i == 0 else (k + dk, v + dv)
    k, v = k.astype(BF16), v.astype(BF16)
    for h in range(H):
        scr[h] = jnp.concatenate([k[h * E:(h + 1) * E], v[h * E:(h + 1) * E]], 0).T
    send_out(me[0], scr, (o0, o1, o2, o3), osem)


def projkv(me, x, wk, wv):
    return call(
        projkv_body, "projkv", 5, (me, x, wk, wv), [sds((NB, 2 * E), BF16)] * 4, [ANY] * 4, [SM, VM, ANY, ANY],
        [pltpu.VMEM((D, HD), BF16), pltpu.VMEM((D, HD), BF16), pltpu.VMEM((H, NB, 2 * E), BF16),
         pltpu.SemaphoreType.DMA((8,)), pltpu.SemaphoreType.DMA((4,))])


def projq_body(me, x, wq, do, o0, o1, o2, o3, wqs, scr, sem, osem):
    cps = loads(((wq, wqs),), sem)
    for c in cps:
        c.start()
    q = None
    doT = do[...].T
    for i in range(4):
        cps[i].wait()
        r = pl.ds(i * KP, KP)
        dq = dot(wqs[r, :], x[:, r], TT)
        q = dq if i == 0 else q + dq
    q = q.astype(BF16)
    for h in range(H):
        scr[h, 0:E, :] = q[h * E:(h + 1) * E]
        scr[h, E:2 * E, :] = doT[h * E:(h + 1) * E]
    send_out(me[0], scr, (o0, o1, o2, o3), osem)


def projq(me, x, wq, do):
    return call(
        projq_body, "projq", 4, (me, x, wq, do), [sds((2 * E, NB), BF16)] * 4, [ANY] * 4, [SM, VM, ANY, VM],
        [pltpu.VMEM((D, HD), BF16), pltpu.VMEM((H, 2 * E, NB), BF16),
         pltpu.SemaphoreType.DMA((4,)), pltpu.SemaphoreType.DMA((4,))])


def pack_body(a, b, c, o):
    for i, p in enumerate((a, b, c)):
        o[i * NB:(i + 1) * NB, :] = p[...]


def pack(a, b, c):
    return call(pack_body, "pack", 1, (a, b, c), sds((3 * NB, 2 * E), BF16), VM, params=SMALL)


def attn_body(core, *refs):
    kv_in, qdo_in = refs[:8], refs[8:12]
    quarters = (refs[14], refs[15], refs[12], refs[13])
    dq_mine, dq_other = refs[16:18]
    dq_out = refs[18:22]
    kv, qdo, qT, doT, s_scr, p_scr, sem = refs[22:]
    cq = [pltpu.make_async_copy(qdo_in[i], qdo.at[:, pl.ds(NB * i, NB)], sem.at[8 + i]) for i in range(4)]
    ck, at = [], 0
    for i in range(8):
        n = NB if i % 2 == 0 else 3 * NB
        ck.append(pltpu.make_async_copy(kv_in[i], kv.at[pl.ds(at, n)], sem.at[i]))
        at += n
    for c in cq + ck:
        c.start()
    for c in cq:
        c.wait()
    zz = jnp.zeros((64, NQ), BF16)
    q, do = qdo[0:E, :], qdo[E:2 * E, :]
    qT[...] = jnp.concatenate([q, zz], 0)
    doT[...] = jnp.concatenate([zz, do], 0)
    m8 = jnp.full((8, NQ), -jnp.inf, F32)
    n = NK // KC
    for i in range(n):
        if i % 2 == 0:
            ck[i].wait()
            ck[i + 1].wait()
        r = pl.ds(i * KC, KC)
        s = dot(kv[r, 0:256], qT[...])
        s_scr[r, :] = s
        m8 = jnp.maximum(m8, jnp.max(s.reshape(KC // 8, 8, NQ), axis=0))
    mc = jnp.max(m8, axis=0, keepdims=True) * C2
    l8 = r8 = jnp.zeros((8, NQ), F32)
    for i in range(n):
        r = pl.ds(i * KC, KC)
        dp = dot(kv[r, 128:384], doT[...])
        p = jnp.exp2(s_scr[r, :] * C2 - mc)
        s_scr[r, :] = dp
        p_scr[r, :] = p.astype(BF16)
        l8 = l8 + jnp.sum(p.reshape(KC // 8, 8, NQ), axis=0)
        r8 = r8 + jnp.sum((p * dp).reshape(KC // 8, 8, NQ), axis=0)
    inv = 1.0 / jnp.sum(l8, axis=0, keepdims=True)
    delta = jnp.sum(r8, axis=0, keepdims=True) * inv
    qs = (q.astype(F32) * (inv * SCALE)).astype(BF16)
    dos = (do.astype(F32) * inv).astype(BF16)
    first = core[0] == 0
    half = n // 2
    acc = None
    for i in list(range(half, n)) + list(range(half)):
        r = pl.ds(i * KC, KC)
        p = p_scr[r, :]
        ds = (p.astype(F32) * (s_scr[r, :] - delta)).astype(BF16)
        dk, dv = nt(qs, ds), nt(dos, p)
        g = dot(kv[r, 0:256].T[:E], ds)
        acc = g if acc is None else acc + g
        at = (i % 2) * KC
        quarters[i // 2][0:E, at:at + KC] = dk.astype(BF16)
        quarters[i // 2][E:2 * E, at:at + KC] = dv.astype(BF16)
    dqT = (acc * (inv * SCALE)).astype(BF16)
    dq_mine[...] = jnp.where(first, dqT[:E // 2], dqT[E // 2:])
    dq_other[...] = jnp.where(first, dqT[E // 2:], dqT[:E // 2])
    for j in range(4):
        dq_out[j][...] = dqT[:, j * NB:(j + 1) * NB]


def attn(core, kvs, qdos):
    part = [sds((2 * E, NQ), BF16)] * 4 + [sds((E // 2, NQ), BF16)] * 2
    return call(
        attn_body, "attn", 1, (core, *kvs, *qdos), part + [sds((E, NB), BF16)] * 4,
        [VM] * 10, [SM] + [ANY] * 12,
        [pltpu.VMEM((NK, 2 * E), BF16), pltpu.VMEM((2 * E, NQ), BF16), pltpu.VMEM((256, NQ), BF16),
         pltpu.VMEM((256, NQ), BF16), pltpu.VMEM((NK, NQ), F32), pltpu.VMEM((NK, NQ), BF16),
         pltpu.SemaphoreType.DMA((12,))])


W = D // 4


def add_body(a, b, o):
    o[...] = (a[...].astype(F32) + b[...].astype(F32)).astype(BF16)


def add(a, b):
    return call(add_body, "add", 1, (a, b), sds(a.shape, BF16), VM, params=SMALL)


def comb_body(core, a, t, u, *refs):
    dqs, ps, mine, other = refs[:4], refs[4:8], refs[8], refs[9]
    d = (a[...].astype(F32) + t[...].astype(F32) + u[...].astype(F32)).astype(BF16)
    for j in range(4):
        ps[j][0:E, :] = dqs[j][...]
        ps[j][E:3 * E, :] = d[:, j * NB:(j + 1) * NB]
    first = core[0] == 0
    mine[...] = jnp.where(first, d[:E], d[E:])
    other[...] = jnp.where(first, d[E:], d[:E])


def comb(core, a, t, u, dqs):
    return call(comb_body, "comb", 1, (core, a, t, u, *dqs), [sds((3 * E, NB), BF16)] * 4 + [sds((E, NQ), BF16)] * 2,
                [VM] * 6, [SM] + [VM] * 7, params=SMALL)


def gkv_body(me, d0, d1, q0, q1, *refs):
    xs, outs, (g, xv, sem) = refs[:8], refs[8:12], refs[12:]
    cps = [pltpu.make_async_copy(x, xv.at[i], sem.at[i]) for i, x in enumerate(xs)]
    for c in cps:
        c.start()
    halves = [jnp.concatenate([d0[...], q0[...]], 0), jnp.concatenate([d1[...], q1[...]], 0)]
    acc = None
    for i in range(8):
        cps[i].wait()
        k = i % 4
        p = dot(halves[i // 4][:, k * NB:(k + 1) * NB], xv[i])
        acc = p if acc is None else acc + p
    g[...] = acc
    for j, o in enumerate(outs):
        at = pl.multiple_of(lax.rem(me[0] + j, 4) * W, 128)
        o[...] = g[:, pl.ds(at, W)].astype(BF16)


def gkv(me, d0, d1, q0, q1, xs):
    n = E + E // 2
    return call(gkv_body, "gkv", 4, (me, d0, d1, q0, q1, *xs), [sds((n, W), BF16)] * 4, [VM] * 4,
                [SM] + [VM] * 4 + [ANY] * 8,
                [pltpu.VMEM((n, D), F32), pltpu.VMEM((8, NB, D), BF16), pltpu.SemaphoreType.DMA((8,))])


def fin1_body(a, b, c, d, out):
    s = ((a[...].astype(F32) + b[...].astype(F32)) + (c[...].astype(F32) + d[...].astype(F32))).T
    for i in range(32):
        out[i] = s[12 * i:12 * i + 12, :].astype(BF16)


def fin1(a):
    return call(fin1_body, "fin1", 1, tuple(a), sds((32, 12, 288), BF16), VM, params=SMALL)


def fin2_body(s, gq_o, gk_o, gv_o):
    for x in range(4):
        for c in range(2):
            v = None
            for zl in range(2):
                for zh in range(2):
                    t = s[((zl * 4 + x) * 2 + zh) * 2 + c].astype(F32)
                    v = t if v is None else v + t
            (gk_o, gv_o)[c][:, x * E:(x + 1) * E] = v[:, :E]
            at = x * E + c * (E // 2)
            gq_o[:, at:at + E // 2] = v[:, E:]


def fin2(s):
    return call(fin2_body, "fin2", 1, (s,), [sds((12, HD), F32)] * 3, [VM] * 3, params=SMALL)


def back_body(count, me, *refs):
    ps, w_in = refs[:4], refs[4:4 + count]
    rest = refs[4 + count:]
    acc = None
    if count == 2:
        acc, rest = rest[0][...], rest[1:]
    out, d, ws, sem = rest
    cps = [pltpu.make_async_copy(w, ws.at[i], sem.at[i]) for i, w in enumerate(w_in)]
    for c in cps:
        c.start()
    for j, p in enumerate(ps):
        at = pl.ds(pl.multiple_of(lax.rem(me[0] + j, H) * E, E), E)
        for i in range(count):
            d[i, at, :] = p[i * E:(i + 1) * E, :]
    for i in range(count):
        x = d[i].T
        cps[i].wait()
        g = nt(x, ws[i])
        acc = g if acc is None else acc + g
    out[...] = acc.astype(out.dtype)


def back(me, ps, ws, *acc):
    n = len(ws)
    return call(functools.partial(back_body, n), "back", 2, (me, *ps, *ws, *acc),
                sds((NB, D), BF16), VM, [SM] + [VM] * 4 + [ANY] * n + [VM] * len(acc),
                [pltpu.VMEM((n, HD, NB), BF16), pltpu.VMEM((n, D, HD), BF16), pltpu.SemaphoreType.DMA((n,))], SMALL)


def ahead(x, axis, j, n):
    return lax.ppermute(x, axis, [(i, (i + j) % n) for i in range(n)])


def core_swap(x):
    return ahead(x, "c", 1, 2)


def around(pieces, axis, sign=1):
    return [pieces[0]] + [ahead(pieces[j], axis, (sign * j) % 4, 4) for j in (1, 2, 3)]


def after(x, y):
    return lax.optimization_barrier((x, y))[0]


def shards(normed, w_query, w_key, w_value, grad_context):
    rows = normed[0]
    cot = grad_context[0]
    mx = lax.axis_index("x").reshape(1)
    my = lax.axis_index("y").reshape(1)
    mc = lax.axis_index("c").reshape(1)
    barrier = lax.optimization_barrier
    kv = projkv(mx, rows, w_key, w_value)
    own0, far0, near0 = kv[0], ahead(kv[0], "zh", 1, 2), core_swap(kv[0])
    kv = around(kv, "x")
    qdo = projq(mx, rows, w_query, cot)
    kv, qdo, far0, near0 = barrier((tuple(kv[1:]), tuple(qdo), far0, near0))
    own = pack(*kv)
    far, near, qdo = barrier((ahead(own, "zh", 1, 2), core_swap(own), tuple(around(qdo, "x"))))
    diag, diag0, rows_n = core_swap(far), core_swap(after(far0, far)), core_swap(after(rows, far))
    x2_from = after(rows, diag)
    xs = [rows, ahead(after(rows, qdo), "x", 1, 4), ahead(x2_from, "x", 2, 4), ahead(after(rows, qdo), "x", 3, 4)]
    diag, diag0, rows_n = barrier((diag, diag0, rows_n))
    kvs = [own0, own, near0, near, far0, far, diag0, diag]
    parts = attn(mc, kvs, qdo)
    parts, x1, x3 = barrier((tuple(parts), xs[1], xs[3]))
    rsame, rother, lsame, lother, dq0, dq1, *dqT = parts
    t, t2 = barrier((core_swap(rother), core_swap(lother)))
    half = add(rsame, t)
    u = ahead(half, "zh", 1, 2)
    x1n, x3n, dqn = barrier(tuple(core_swap(after(v, half)) for v in (x1, x3, dq1)))
    x2n = core_swap(after(xs[2], x1n))
    u, t2, x2n, x1n, x3n, dqn = barrier((u, t2, x2n, x1n, x3n, dqn))
    *ps, dmine, dother = comb(mc, lsame, t2, u, dqT)
    ps = around(ps, "x", -1)
    s4 = gkv(my, dmine, core_swap(dother), dq0, dqn, [rows, x1, xs[2], x3, rows_n, x1n, x2n, x3n])
    s4, ps = barrier((tuple(s4), tuple(ps)))
    s4 = around(s4, "y")
    out = back(mx, ps, [w_query, w_key, w_value])
    s4, out = barrier((tuple(s4), out))
    d_normed = out.reshape(normed.shape)
    s = lax.all_to_all(fin1(s4), ("zl", "x", "zh", "c"), 0, 0, tiled=True)
    grad_q, grad_k, grad_v = fin2(s)
    return d_normed, grad_q, grad_k, grad_v


def solution(mesh):
    split_mesh = Mesh(mesh.devices.reshape(4, 2, 4, 2, 2), ("y", "zl", "x", "zh", "c"))
    dp, seq = ("y", "zl"), ("x", "zh", "c")
    rows = P(dp, seq, None)
    grads = P(dp + seq, None)
    return jax.shard_map(
        shards, mesh=split_mesh, in_specs=(rows, P(), P(), P(), rows),
        out_specs=(rows, grads, grads, grads), check_vma=False,
    )
```

```python
import functools
import math

import jax
import jax.numpy as jnp
from jax import lax
from jax.experimental import pallas as pl
from jax.experimental.pallas import tpu as pltpu
from jax.sharding import Mesh, PartitionSpec as P

F32, BF16 = jnp.float32, jnp.bfloat16
D = 1536
H = 4
E = 192
HD = H * E
NB = 256
NQ = 4 * NB
NK = 16 * NB
KC = 512
SCALE = 1.0 / math.sqrt(E)
C2 = SCALE * math.log2(math.e)
ANY = pl.BlockSpec(memory_space=pl.ANY)
VM = pl.BlockSpec(memory_space=pltpu.VMEM)
SM = pl.BlockSpec(memory_space=pltpu.SMEM)
PARAMS = pltpu.CompilerParams(vmem_limit_bytes=58 * 2**20)
SMALL = pltpu.CompilerParams(vmem_limit_bytes=24 * 2**20)
sds = jax.ShapeDtypeStruct


def dot(a, b, dims=(((1,), (0,)), ((), ()))):
    return lax.dot_general(a, b, dims, preferred_element_type=F32)


def nt(a, b):
    return dot(a, b, (((1,), (1,)), ((), ())))


def call(body, name, us, ins, outs, out_specs, in_specs=None, scratch=(), params=PARAMS):
    return pl.pallas_call(
        body, in_specs=in_specs or [VM] * len(ins), out_specs=out_specs, out_shape=outs,
        scratch_shapes=list(scratch), compiler_params=params, name=name,
        cost_estimate=pl.CostEstimate(flops=2**20, bytes_accessed=int(us * 1e5), transcendentals=0),
    )(*ins)


KP = D // 4


def send_out(me, scr, outs, sem):
    cps = [pltpu.make_async_copy(scr.at[lax.rem(me + j, H)], outs[j], sem.at[j]) for j in range(4)]
    for c in cps:
        c.start()
    for c in cps:
        c.wait()


def loads(pairs, sem):
    cps = []
    for n, (a, b) in enumerate(pairs):
        for i in range(4):
            r = pl.ds(i * KP, KP)
            cps.append(pltpu.make_async_copy(a.at[r], b.at[r], sem.at[4 * n + i]))
    return cps


TT = (((0,), (1,)), ((), ()))


def projkv_body(me, x, wk, wv, o0, o1, o2, o3, wks, wvs, scr, sem, osem):
    cps = loads(((wk, wks), (wv, wvs)), sem)
    for i in range(4):
        cps[i].start()
        cps[4 + i].start()
    k = v = None
    for i in range(4):
        cps[i].wait()
        cps[4 + i].wait()
        r = pl.ds(i * KP, KP)
        xi = x[:, r]
        dk, dv = dot(wks[r, :], xi, TT), dot(wvs[r, :], xi, TT)
        k, v = (dk, dv) if i == 0 else (k + dk, v + dv)
    k, v = k.astype(BF16), v.astype(BF16)
    for h in range(H):
        scr[h] = jnp.concatenate([k[h * E:(h + 1) * E], v[h * E:(h + 1) * E]], 0).T
    send_out(me[0], scr, (o0, o1, o2, o3), osem)


def projkv(me, x, wk, wv):
    return call(
        projkv_body, "projkv", 5, (me, x, wk, wv), [sds((NB, 2 * E), BF16)] * 4, [ANY] * 4, [SM, VM, ANY, ANY],
        [pltpu.VMEM((D, HD), BF16), pltpu.VMEM((D, HD), BF16), pltpu.VMEM((H, NB, 2 * E), BF16),
         pltpu.SemaphoreType.DMA((8,)), pltpu.SemaphoreType.DMA((4,))])


def projq_body(me, x, wq, do, o0, o1, o2, o3, wqs, scr, sem, osem):
    cps = loads(((wq, wqs),), sem)
    for c in cps:
        c.start()
    q = None
    doT = do[...].T
    for i in range(4):
        cps[i].wait()
        r = pl.ds(i * KP, KP)
        dq = dot(wqs[r, :], x[:, r], TT)
        q = dq if i == 0 else q + dq
    q = q.astype(BF16)
    for h in range(H):
        scr[h, 0:E, :] = q[h * E:(h + 1) * E]
        scr[h, E:2 * E, :] = doT[h * E:(h + 1) * E]
    send_out(me[0], scr, (o0, o1, o2, o3), osem)


def projq(me, x, wq, do):
    return call(
        projq_body, "projq", 4, (me, x, wq, do), [sds((2 * E, NB), BF16)] * 4, [ANY] * 4, [SM, VM, ANY, VM],
        [pltpu.VMEM((D, HD), BF16), pltpu.VMEM((H, 2 * E, NB), BF16),
         pltpu.SemaphoreType.DMA((4,)), pltpu.SemaphoreType.DMA((4,))])


def pack_body(a, b, c, o):
    for i, p in enumerate((a, b, c)):
        o[i * NB:(i + 1) * NB, :] = p[...]


def pack(a, b, c):
    return call(pack_body, "pack", 1, (a, b, c), sds((3 * NB, 2 * E), BF16), VM, params=SMALL)


def attn_body(core, *refs):
    kv_in, qdo_in = refs[:8], refs[8:12]
    quarters = (refs[14], refs[15], refs[12], refs[13])
    dq_mine, dq_other = refs[16:18]
    dq_out = refs[18:22]
    kv, qdo, qT, doT, s_scr, p_scr, sem = refs[22:]
    cq = [pltpu.make_async_copy(qdo_in[i], qdo.at[:, pl.ds(NB * i, NB)], sem.at[8 + i]) for i in range(4)]
    ck, at = [], 0
    for i in range(8):
        n = NB if i % 2 == 0 else 3 * NB
        ck.append(pltpu.make_async_copy(kv_in[i], kv.at[pl.ds(at, n)], sem.at[i]))
        at += n
    for c in cq + ck:
        c.start()
    for c in cq:
        c.wait()
    zz = jnp.zeros((64, NQ), BF16)
    q, do = qdo[0:E, :], qdo[E:2 * E, :]
    qT[...] = jnp.concatenate([q, zz], 0)
    doT[...] = jnp.concatenate([zz, do], 0)
    m8 = jnp.full((8, NQ), -jnp.inf, F32)
    n = NK // KC
    for i in range(n):
        if i % 2 == 0:
            ck[i].wait()
            ck[i + 1].wait()
        r = pl.ds(i * KC, KC)
        s = dot(kv[r, 0:256], qT[...])
        s_scr[r, :] = s
        m8 = jnp.maximum(m8, jnp.max(s.reshape(KC // 8, 8, NQ), axis=0))
    mc = jnp.max(m8, axis=0, keepdims=True) * C2
    l8 = r8 = jnp.zeros((8, NQ), F32)
    for i in range(n):
        r = pl.ds(i * KC, KC)
        dp = dot(kv[r, 128:384], doT[...])
        p = jnp.exp2(s_scr[r, :] * C2 - mc)
        s_scr[r, :] = dp
        p_scr[r, :] = p.astype(BF16)
        l8 = l8 + jnp.sum(p.reshape(KC // 8, 8, NQ), axis=0)
        r8 = r8 + jnp.sum((p * dp).reshape(KC // 8, 8, NQ), axis=0)
    inv = 1.0 / jnp.sum(l8, axis=0, keepdims=True)
    delta = jnp.sum(r8, axis=0, keepdims=True) * inv
    qs = (q.astype(F32) * (inv * SCALE)).astype(BF16)
    dos = (do.astype(F32) * inv).astype(BF16)
    first = core[0] == 0
    half = n // 2
    acc = None
    for i in list(range(half, n)) + list(range(half)):
        r = pl.ds(i * KC, KC)
        p = p_scr[r, :]
        ds = (p.astype(F32) * (s_scr[r, :] - delta)).astype(BF16)
        dk, dv = nt(qs, ds), nt(dos, p)
        g = dot(kv[r, 0:256].T[:E], ds)
        acc = g if acc is None else acc + g
        at = (i % 2) * KC
        quarters[i // 2][0:E, at:at + KC] = dk.astype(BF16)
        quarters[i // 2][E:2 * E, at:at + KC] = dv.astype(BF16)
    dqT = (acc * (inv * SCALE)).astype(BF16)
    dq_mine[...] = jnp.where(first, dqT[:E // 2], dqT[E // 2:])
    dq_other[...] = jnp.where(first, dqT[E // 2:], dqT[:E // 2])
    for j in range(4):
        dq_out[j][...] = dqT[:, j * NB:(j + 1) * NB]


def attn(core, kvs, qdos):
    part = [sds((2 * E, NQ), BF16)] * 4 + [sds((E // 2, NQ), BF16)] * 2
    return call(
        attn_body, "attn", 1, (core, *kvs, *qdos), part + [sds((E, NB), BF16)] * 4,
        [VM] * 10, [SM] + [ANY] * 12,
        [pltpu.VMEM((NK, 2 * E), BF16), pltpu.VMEM((2 * E, NQ), BF16), pltpu.VMEM((256, NQ), BF16),
         pltpu.VMEM((256, NQ), BF16), pltpu.VMEM((NK, NQ), F32), pltpu.VMEM((NK, NQ), BF16),
         pltpu.SemaphoreType.DMA((12,))])


W = D // 4


def add_body(a, b, o):
    o[...] = (a[...].astype(F32) + b[...].astype(F32)).astype(BF16)


def add(a, b):
    return call(add_body, "add", 1, (a, b), sds(a.shape, BF16), VM, params=SMALL)


def comb_body(core, a, t, u, *refs):
    dqs, ps, mine, other = refs[:4], refs[4:8], refs[8], refs[9]
    d = (a[...].astype(F32) + t[...].astype(F32) + u[...].astype(F32)).astype(BF16)
    for j in range(4):
        ps[j][0:E, :] = dqs[j][...]
        ps[j][E:3 * E, :] = d[:, j * NB:(j + 1) * NB]
    first = core[0] == 0
    mine[...] = jnp.where(first, d[:E], d[E:])
    other[...] = jnp.where(first, d[E:], d[:E])


def comb(core, a, t, u, dqs):
    return call(comb_body, "comb", 1, (core, a, t, u, *dqs), [sds((3 * E, NB), BF16)] * 4 + [sds((E, NQ), BF16)] * 2,
                [VM] * 6, [SM] + [VM] * 7, params=SMALL)


def gkv_body(me, d0, d1, q0, q1, *refs):
    xs, outs, (g, xv, sem) = refs[:8], refs[8:12], refs[12:]
    cps = [pltpu.make_async_copy(x, xv.at[i], sem.at[i]) for i, x in enumerate(xs)]
    for c in cps:
        c.start()
    halves = [jnp.concatenate([d0[...], q0[...]], 0), jnp.concatenate([d1[...], q1[...]], 0)]
    acc = None
    for i in range(8):
        cps[i].wait()
        k = i % 4
        p = dot(halves[i // 4][:, k * NB:(k + 1) * NB], xv[i])
        acc = p if acc is None else acc + p
    g[...] = acc
    for j, o in enumerate(outs):
        at = pl.multiple_of(lax.rem(me[0] + j, 4) * W, 128)
        o[...] = g[:, pl.ds(at, W)].astype(BF16)


def gkv(me, d0, d1, q0, q1, xs):
    n = E + E // 2
    return call(gkv_body, "gkv", 4, (me, d0, d1, q0, q1, *xs), [sds((n, W), BF16)] * 4, [VM] * 4,
                [SM] + [VM] * 4 + [ANY] * 8,
                [pltpu.VMEM((n, D), F32), pltpu.VMEM((8, NB, D), BF16), pltpu.SemaphoreType.DMA((8,))])


def fin1_body(a, b, c, d, out):
    s = ((a[...].astype(F32) + b[...].astype(F32)) + (c[...].astype(F32) + d[...].astype(F32))).T
    for i in range(32):
        out[i] = s[12 * i:12 * i + 12, :].astype(BF16)


def fin1(a):
    return call(fin1_body, "fin1", 1, tuple(a), sds((32, 12, 288), BF16), VM, params=SMALL)


def fin2_body(s, gq_o, gk_o, gv_o):
    for x in range(4):
        for c in range(2):
            v = None
            for zl in range(2):
                for zh in range(2):
                    t = s[((zl * 4 + x) * 2 + zh) * 2 + c].astype(F32)
                    v = t if v is None else v + t
            (gk_o, gv_o)[c][:, x * E:(x + 1) * E] = v[:, :E]
            at = x * E + c * (E // 2)
            gq_o[:, at:at + E // 2] = v[:, E:]


def fin2(s):
    return call(fin2_body, "fin2", 1, (s,), [sds((12, HD), F32)] * 3, [VM] * 3, params=SMALL)


def back_body(count, me, *refs):
    ps, w_in = refs[:4], refs[4:4 + count]
    rest = refs[4 + count:]
    acc = None
    if count == 2:
        acc, rest = rest[0][...], rest[1:]
    out, d, ws, sem = rest
    cps = [pltpu.make_async_copy(w, ws.at[i], sem.at[i]) for i, w in enumerate(w_in)]
    for c in cps:
        c.start()
    for j, p in enumerate(ps):
        at = pl.ds(pl.multiple_of(lax.rem(me[0] + j, H) * E, E), E)
        for i in range(count):
            d[i, at, :] = p[i * E:(i + 1) * E, :]
    for i in range(count):
        x = d[i].T
        cps[i].wait()
        g = nt(x, ws[i])
        acc = g if acc is None else acc + g
    out[...] = acc.astype(out.dtype)


def back(me, ps, ws, *acc):
    n = len(ws)
    return call(functools.partial(back_body, n), "back", 2, (me, *ps, *ws, *acc),
                sds((NB, D), BF16), VM, [SM] + [VM] * 4 + [ANY] * n + [VM] * len(acc),
                [pltpu.VMEM((n, HD, NB), BF16), pltpu.VMEM((n, D, HD), BF16), pltpu.SemaphoreType.DMA((n,))], SMALL)


def ahead(x, axis, j, n):
    return lax.ppermute(x, axis, [(i, (i + j) % n) for i in range(n)])


def core_swap(x):
    return ahead(x, "c", 1, 2)


def around(pieces, axis, sign=1):
    return [pieces[0]] + [ahead(pieces[j], axis, (sign * j) % 4, 4) for j in (1, 2, 3)]


def after(x, y):
    return lax.optimization_barrier((x, y))[0]


def shards(normed, w_query, w_key, w_value, grad_context):
    rows = normed[0]
    cot = grad_context[0]
    mx = lax.axis_index("x").reshape(1)
    my = lax.axis_index("y").reshape(1)
    mc = lax.axis_index("c").reshape(1)
    barrier = lax.optimization_barrier
    kv = projkv(mx, rows, w_key, w_value)
    own0, far0, near0 = kv[0], ahead(kv[0], "zh", 1, 2), core_swap(kv[0])
    kv = around(kv, "x")
    qdo = projq(mx, rows, w_query, cot)
    kv, qdo, far0, near0 = barrier((tuple(kv[1:]), tuple(qdo), far0, near0))
    own = pack(*kv)
    far, near, qdo = barrier((ahead(own, "zh", 1, 2), core_swap(own), tuple(around(qdo, "x"))))
    diag, diag0, rows_n = core_swap(far), core_swap(after(far0, far)), core_swap(after(rows, far))
    x2_from = after(rows, diag)
    xs = [rows, ahead(after(rows, qdo), "x", 1, 4), ahead(x2_from, "x", 2, 4), ahead(after(rows, qdo), "x", 3, 4)]
    diag, diag0, rows_n = barrier((diag, diag0, rows_n))
    kvs = [own0, own, near0, near, far0, far, diag0, diag]
    parts = attn(mc, kvs, qdo)
    parts, x1, x3 = barrier((tuple(parts), xs[1], xs[3]))
    rsame, rother, lsame, lother, dq0, dq1, *dqT = parts
    t, t2 = barrier((core_swap(rother), core_swap(lother)))
    half = add(rsame, t)
    u = ahead(half, "zh", 1, 2)
    x1n, x3n, dqn = barrier(tuple(core_swap(after(v, half)) for v in (x1, x3, dq1)))
    u, t2, x1n, x3n, dqn = barrier((u, t2, x1n, x3n, dqn))
    x2n = core_swap(after(xs[2], u))
    *ps, dmine, dother = comb(mc, lsame, t2, u, dqT)
    ps = around(ps, "x", -1)
    s4 = gkv(my, dmine, core_swap(dother), dq0, dqn, [rows, x1, xs[2], x3, rows_n, x1n, x2n, x3n])
    s4, ps1, ps2 = barrier((tuple(s4), ps[1], ps[2]))
    ps = [ps[0], ps1, ps2, ps[3]]
    s4 = around(s4, "y")
    out = back(mx, ps, [w_query, w_key, w_value])
    s4, out = barrier((tuple(s4), out))
    d_normed = out.reshape(normed.shape)
    s = lax.all_to_all(fin1(s4), ("zl", "x", "zh", "c"), 0, 0, tiled=True)
    grad_q, grad_k, grad_v = fin2(s)
    return d_normed, grad_q, grad_k, grad_v


def solution(mesh):
    split_mesh = Mesh(mesh.devices.reshape(4, 2, 4, 2, 2), ("y", "zl", "x", "zh", "c"))
    dp, seq = ("y", "zl"), ("x", "zh", "c")
    rows = P(dp, seq, None)
    grads = P(dp + seq, None)
    return jax.shard_map(
        shards, mesh=split_mesh, in_specs=(rows, P(), P(), P(), rows),
        out_specs=(rows, grads, grads, grads), check_vma=False,
    )
```

```python
import functools
import math

import jax
import jax.numpy as jnp
from jax import lax
from jax.experimental import pallas as pl
from jax.experimental.pallas import tpu as pltpu
from jax.sharding import Mesh, PartitionSpec as P

F32, BF16 = jnp.float32, jnp.bfloat16
D = 1536
H = 4
E = 192
HD = H * E
NB = 256
NQ = 4 * NB
NK = 16 * NB
KC = 512
SCALE = 1.0 / math.sqrt(E)
C2 = SCALE * math.log2(math.e)
ANY = pl.BlockSpec(memory_space=pl.ANY)
VM = pl.BlockSpec(memory_space=pltpu.VMEM)
SM = pl.BlockSpec(memory_space=pltpu.SMEM)
PARAMS = pltpu.CompilerParams(vmem_limit_bytes=58 * 2**20)
SMALL = pltpu.CompilerParams(vmem_limit_bytes=24 * 2**20)
sds = jax.ShapeDtypeStruct


def dot(a, b, dims=(((1,), (0,)), ((), ()))):
    return lax.dot_general(a, b, dims, preferred_element_type=F32)


def nt(a, b):
    return dot(a, b, (((1,), (1,)), ((), ())))


def call(body, name, us, ins, outs, out_specs, in_specs=None, scratch=(), params=PARAMS):
    return pl.pallas_call(
        body, in_specs=in_specs or [VM] * len(ins), out_specs=out_specs, out_shape=outs,
        scratch_shapes=list(scratch), compiler_params=params, name=name,
        cost_estimate=pl.CostEstimate(flops=2**20, bytes_accessed=int(us * 1e5), transcendentals=0),
    )(*ins)


KP = D // 4


def send_out(me, scr, outs, sem):
    cps = [pltpu.make_async_copy(scr.at[lax.rem(me + j, H)], outs[j], sem.at[j]) for j in range(4)]
    for c in cps:
        c.start()
    for c in cps:
        c.wait()


def loads(pairs, sem):
    cps = []
    for n, (a, b) in enumerate(pairs):
        for i in range(4):
            r = pl.ds(i * KP, KP)
            cps.append(pltpu.make_async_copy(a.at[r], b.at[r], sem.at[4 * n + i]))
    return cps


TT = (((0,), (1,)), ((), ()))


def projkv_body(me, x_in, wk, wv, o0, o1, o2, o3, x, wks, wvs, scr, sem, osem, xsem):
    cx = pltpu.make_async_copy(x_in, x, xsem.at[0])
    cx.start()
    cps = loads(((wk, wks), (wv, wvs)), sem)
    for i in range(4):
        cps[i].start()
        cps[4 + i].start()
    cx.wait()
    k = v = None
    for i in range(4):
        cps[i].wait()
        cps[4 + i].wait()
        r = pl.ds(i * KP, KP)
        xi = x[:, r]
        dk, dv = dot(wks[r, :], xi, TT), dot(wvs[r, :], xi, TT)
        k, v = (dk, dv) if i == 0 else (k + dk, v + dv)
    k, v = k.astype(BF16), v.astype(BF16)
    for h in range(H):
        scr[h] = jnp.concatenate([k[h * E:(h + 1) * E], v[h * E:(h + 1) * E]], 0).T
    send_out(me[0], scr, (o0, o1, o2, o3), osem)


def projkv(me, x, wk, wv):
    return call(
        projkv_body, "projkv", 5, (me, x, wk, wv), [sds((NB, 2 * E), BF16)] * 4, [ANY] * 4, [SM, ANY, ANY, ANY],
        [pltpu.VMEM((NB, D), BF16), pltpu.VMEM((D, HD), BF16), pltpu.VMEM((D, HD), BF16),
         pltpu.VMEM((H, NB, 2 * E), BF16),
         pltpu.SemaphoreType.DMA((8,)), pltpu.SemaphoreType.DMA((4,)), pltpu.SemaphoreType.DMA((1,))])


def projq_body(me, x, wq, do, o0, o1, o2, o3, wqs, scr, sem, osem):
    cps = loads(((wq, wqs),), sem)
    for c in cps:
        c.start()
    q = None
    doT = do[...].T
    for i in range(4):
        cps[i].wait()
        r = pl.ds(i * KP, KP)
        dq = dot(wqs[r, :], x[:, r], TT)
        q = dq if i == 0 else q + dq
    q = q.astype(BF16)
    for h in range(H):
        scr[h, 0:E, :] = q[h * E:(h + 1) * E]
        scr[h, E:2 * E, :] = doT[h * E:(h + 1) * E]
    send_out(me[0], scr, (o0, o1, o2, o3), osem)


def projq(me, x, wq, do):
    return call(
        projq_body, "projq", 4, (me, x, wq, do), [sds((2 * E, NB), BF16)] * 4, [ANY] * 4, [SM, VM, ANY, VM],
        [pltpu.VMEM((D, HD), BF16), pltpu.VMEM((H, 2 * E, NB), BF16),
         pltpu.SemaphoreType.DMA((4,)), pltpu.SemaphoreType.DMA((4,))])


def pack_body(a, b, c, o):
    for i, p in enumerate((a, b, c)):
        o[i * NB:(i + 1) * NB, :] = p[...]


def pack(a, b, c):
    return call(pack_body, "pack", 1, (a, b, c), sds((3 * NB, 2 * E), BF16), VM, params=SMALL)


def attn_body(core, *refs):
    kv_in, qdo_in = refs[:8], refs[8:12]
    quarters = (refs[14], refs[15], refs[12], refs[13])
    dq_mine, dq_other = refs[16:18]
    dq_out = refs[18:22]
    kv, qdo, qT, doT, s_scr, p_scr, sem = refs[22:]
    cq = [pltpu.make_async_copy(qdo_in[i], qdo.at[:, pl.ds(NB * i, NB)], sem.at[8 + i]) for i in range(4)]
    ck, at = [], 0
    for i in range(8):
        n = NB if i % 2 == 0 else 3 * NB
        ck.append(pltpu.make_async_copy(kv_in[i], kv.at[pl.ds(at, n)], sem.at[i]))
        at += n
    for c in cq + ck:
        c.start()
    for c in cq:
        c.wait()
    zz = jnp.zeros((64, NQ), BF16)
    q, do = qdo[0:E, :], qdo[E:2 * E, :]
    qT[...] = jnp.concatenate([q, zz], 0)
    doT[...] = jnp.concatenate([zz, do], 0)
    m8 = jnp.full((8, NQ), -jnp.inf, F32)
    n = NK // KC
    for i in range(n):
        if i % 2 == 0:
            ck[i].wait()
            ck[i + 1].wait()
        r = pl.ds(i * KC, KC)
        s = dot(kv[r, 0:256], qT[...])
        s_scr[r, :] = s
        m8 = jnp.maximum(m8, jnp.max(s.reshape(KC // 8, 8, NQ), axis=0))
    mc = jnp.max(m8, axis=0, keepdims=True) * C2
    l8 = r8 = jnp.zeros((8, NQ), F32)
    for i in range(n):
        r = pl.ds(i * KC, KC)
        dp = dot(kv[r, 128:384], doT[...])
        p = jnp.exp2(s_scr[r, :] * C2 - mc)
        s_scr[r, :] = dp
        p_scr[r, :] = p.astype(BF16)
        l8 = l8 + jnp.sum(p.reshape(KC // 8, 8, NQ), axis=0)
        r8 = r8 + jnp.sum((p * dp).reshape(KC // 8, 8, NQ), axis=0)
    inv = 1.0 / jnp.sum(l8, axis=0, keepdims=True)
    delta = jnp.sum(r8, axis=0, keepdims=True) * inv
    qs = (q.astype(F32) * (inv * SCALE)).astype(BF16)
    dos = (do.astype(F32) * inv).astype(BF16)
    first = core[0] == 0
    half = n // 2
    acc = None
    for i in list(range(half, n)) + list(range(half)):
        r = pl.ds(i * KC, KC)
        p = p_scr[r, :]
        ds = (p.astype(F32) * (s_scr[r, :] - delta)).astype(BF16)
        dk, dv = nt(qs, ds), nt(dos, p)
        g = dot(kv[r, 0:256].T[:E], ds)
        acc = g if acc is None else acc + g
        at = (i % 2) * KC
        quarters[i // 2][0:E, at:at + KC] = dk.astype(BF16)
        quarters[i // 2][E:2 * E, at:at + KC] = dv.astype(BF16)
    dqT = (acc * (inv * SCALE)).astype(BF16)
    dq_mine[...] = jnp.where(first, dqT[:E // 2], dqT[E // 2:])
    dq_other[...] = jnp.where(first, dqT[E // 2:], dqT[:E // 2])
    for j in range(4):
        dq_out[j][...] = dqT[:, j * NB:(j + 1) * NB]


def attn(core, kvs, qdos):
    part = [sds((2 * E, NQ), BF16)] * 4 + [sds((E // 2, NQ), BF16)] * 2
    return call(
        attn_body, "attn", 1, (core, *kvs, *qdos), part + [sds((E, NB), BF16)] * 4,
        [VM] * 10, [SM] + [ANY] * 12,
        [pltpu.VMEM((NK, 2 * E), BF16), pltpu.VMEM((2 * E, NQ), BF16), pltpu.VMEM((256, NQ), BF16),
         pltpu.VMEM((256, NQ), BF16), pltpu.VMEM((NK, NQ), F32), pltpu.VMEM((NK, NQ), BF16),
         pltpu.SemaphoreType.DMA((12,))])


W = D // 4


def add_body(a, b, o):
    o[...] = (a[...].astype(F32) + b[...].astype(F32)).astype(BF16)


def add(a, b):
    return call(add_body, "add", 1, (a, b), sds(a.shape, BF16), VM, params=SMALL)


def comb_body(core, a, t, u, *refs):
    dqs, ps, mine, other = refs[:4], refs[4:8], refs[8], refs[9]
    d = (a[...].astype(F32) + t[...].astype(F32) + u[...].astype(F32)).astype(BF16)
    for j in range(4):
        ps[j][0:E, :] = dqs[j][...]
        ps[j][E:3 * E, :] = d[:, j * NB:(j + 1) * NB]
    first = core[0] == 0
    mine[...] = jnp.where(first, d[:E], d[E:])
    other[...] = jnp.where(first, d[E:], d[:E])


def comb(core, a, t, u, dqs):
    return call(comb_body, "comb", 1, (core, a, t, u, *dqs), [sds((3 * E, NB), BF16)] * 4 + [sds((E, NQ), BF16)] * 2,
                [VM] * 6, [SM] + [VM] * 7, params=SMALL)


def gkv_body(me, d0, d1, q0, q1, *refs):
    xs, outs, (g, xv, sem) = refs[:8], refs[8:12], refs[12:]
    cps = [pltpu.make_async_copy(x, xv.at[i], sem.at[i]) for i, x in enumerate(xs)]
    for c in cps:
        c.start()
    halves = [jnp.concatenate([d0[...], q0[...]], 0), jnp.concatenate([d1[...], q1[...]], 0)]
    acc = None
    for i in range(8):
        cps[i].wait()
        k = i % 4
        p = dot(halves[i // 4][:, k * NB:(k + 1) * NB], xv[i])
        acc = p if acc is None else acc + p
    g[...] = acc
    for j, o in enumerate(outs):
        at = pl.multiple_of(lax.rem(me[0] + j, 4) * W, 128)
        o[...] = g[:, pl.ds(at, W)].astype(BF16)


def gkv(me, d0, d1, q0, q1, xs):
    n = E + E // 2
    return call(gkv_body, "gkv", 4, (me, d0, d1, q0, q1, *xs), [sds((n, W), BF16)] * 4, [VM] * 4,
                [SM] + [VM] * 4 + [ANY] * 8,
                [pltpu.VMEM((n, D), F32), pltpu.VMEM((8, NB, D), BF16), pltpu.SemaphoreType.DMA((8,))])


def fin1_body(a, b, c, d, out):
    s = ((a[...].astype(F32) + b[...].astype(F32)) + (c[...].astype(F32) + d[...].astype(F32))).T
    for i in range(32):
        out[i] = s[12 * i:12 * i + 12, :].astype(BF16)


def fin1(a):
    return call(fin1_body, "fin1", 1, tuple(a), sds((32, 12, 288), BF16), VM, params=SMALL)


def fin2_body(s, gq_o, gk_o, gv_o):
    for x in range(4):
        for c in range(2):
            v = None
            for zl in range(2):
                for zh in range(2):
                    t = s[((zl * 4 + x) * 2 + zh) * 2 + c].astype(F32)
                    v = t if v is None else v + t
            (gk_o, gv_o)[c][:, x * E:(x + 1) * E] = v[:, :E]
            at = x * E + c * (E // 2)
            gq_o[:, at:at + E // 2] = v[:, E:]


def fin2(s):
    return call(fin2_body, "fin2", 1, (s,), [sds((12, HD), F32)] * 3, [VM] * 3, params=SMALL)


def back_body(count, me, *refs):
    ps, w_in = refs[:4], refs[4:4 + count]
    rest = refs[4 + count:]
    acc = None
    if count == 2:
        acc, rest = rest[0][...], rest[1:]
    out, d, ws, sem = rest
    cps = [pltpu.make_async_copy(w, ws.at[i], sem.at[i]) for i, w in enumerate(w_in)]
    for c in cps:
        c.start()
    for j, p in enumerate(ps):
        at = pl.ds(pl.multiple_of(lax.rem(me[0] + j, H) * E, E), E)
        for i in range(count):
            d[i, at, :] = p[i * E:(i + 1) * E, :]
    for i in range(count):
        x = d[i].T
        cps[i].wait()
        g = nt(x, ws[i])
        acc = g if acc is None else acc + g
    out[...] = acc.astype(out.dtype)


def back(me, ps, ws, *acc):
    n = len(ws)
    return call(functools.partial(back_body, n), "back", 2, (me, *ps, *ws, *acc),
                sds((NB, D), BF16), VM, [SM] + [VM] * 4 + [ANY] * n + [VM] * len(acc),
                [pltpu.VMEM((n, HD, NB), BF16), pltpu.VMEM((n, D, HD), BF16), pltpu.SemaphoreType.DMA((n,))], SMALL)


def ahead(x, axis, j, n):
    return lax.ppermute(x, axis, [(i, (i + j) % n) for i in range(n)])


def core_swap(x):
    return ahead(x, "c", 1, 2)


def around(pieces, axis, sign=1):
    return [pieces[0]] + [ahead(pieces[j], axis, (sign * j) % 4, 4) for j in (1, 2, 3)]


def after(x, y):
    return lax.optimization_barrier((x, y))[0]


def shards(normed, w_query, w_key, w_value, grad_context):
    rows = normed[0]
    cot = grad_context[0]
    mx = lax.axis_index("x").reshape(1)
    my = lax.axis_index("y").reshape(1)
    mc = lax.axis_index("c").reshape(1)
    barrier = lax.optimization_barrier
    kv = projkv(mx, rows, w_key, w_value)
    own0, far0, near0 = kv[0], ahead(kv[0], "zh", 1, 2), core_swap(kv[0])
    kv = around(kv, "x")
    qdo = projq(mx, rows, w_query, cot)
    kv, qdo, far0, near0 = barrier((tuple(kv[1:]), tuple(qdo), far0, near0))
    own = pack(*kv)
    far, near, qdo = barrier((ahead(own, "zh", 1, 2), core_swap(own), tuple(around(qdo, "x"))))
    diag, diag0, rows_n = core_swap(far), core_swap(after(far0, far)), core_swap(after(rows, far))
    x2_from = after(rows, diag)
    xs = [rows, ahead(after(rows, qdo), "x", 1, 4), ahead(x2_from, "x", 2, 4), ahead(after(rows, qdo), "x", 3, 4)]
    diag, diag0, rows_n = barrier((diag, diag0, rows_n))
    kvs = [own0, own, near0, near, far0, far, diag0, diag]
    parts = attn(mc, kvs, qdo)
    parts, x1, x3 = barrier((tuple(parts), xs[1], xs[3]))
    rsame, rother, lsame, lother, dq0, dq1, *dqT = parts
    t, t2 = barrier((core_swap(rother), core_swap(lother)))
    half = add(rsame, t)
    u = ahead(half, "zh", 1, 2)
    x1n, x3n, dqn = barrier(tuple(core_swap(after(v, half)) for v in (x1, x3, dq1)))
    u, t2, x1n, x3n, dqn = barrier((u, t2, x1n, x3n, dqn))
    x2n = core_swap(after(xs[2], u))
    *ps, dmine, dother = comb(mc, lsame, t2, u, dqT)
    ps = around(ps, "x", -1)
    s4 = gkv(my, dmine, core_swap(dother), dq0, dqn, [rows, x1, xs[2], x3, rows_n, x1n, x2n, x3n])
    s4, ps2 = barrier((tuple(s4), ps[2]))
    ps = [ps[0], ps[1], ps2, ps[3]]
    s4 = around(s4, "y")
    out = back(mx, ps, [w_query, w_key, w_value])
    s4, out = barrier((tuple(s4), out))
    d_normed = out.reshape(normed.shape)
    s = lax.all_to_all(fin1(s4), ("zl", "x", "zh", "c"), 0, 0, tiled=True)
    grad_q, grad_k, grad_v = fin2(s)
    return d_normed, grad_q, grad_k, grad_v


def solution(mesh):
    split_mesh = Mesh(mesh.devices.reshape(4, 2, 4, 2, 2), ("y", "zl", "x", "zh", "c"))
    dp, seq = ("y", "zl"), ("x", "zh", "c")
    rows = P(dp, seq, None)
    grads = P(dp + seq, None)
    return jax.shard_map(
        shards, mesh=split_mesh, in_specs=(rows, P(), P(), P(), rows),
        out_specs=(rows, grads, grads, grads), check_vma=False,
    )
```
